512 devices in a mesh: ex: 64 (over x_hi, z, core), feat: 8 (over y, x_lo).
Axes of the slice: x: 4 (x_hi: 2, x_lo: 2; x = x_hi * 2 + x_lo), y: 4, z: 16, core: 2. Of those that a mesh axis runs over, the one named last changes fastest.
Arguments:
- features: bfloat16 [6144, 8192], P('ex', 'feat'), may hold values from -100 to 100
Outputs:
- kernel: float32 [6144, 6144], P('ex', 'feat')
The draws below stay inside these ranges and needn't reach their ends.
All inputs are finite; a program needn't handle non-finite values.
Results may differ from the reference program's by a relative error of at most 0.0003.
Values may be sent and summed in bfloat16 or wider, within the bound.
No kernel may reach another device: no remote copies, remote signals or barrier semaphores. Data moves between devices by JAX's collectives and lax.ppermute only.
A program may use at most 64 MiB of HBM per device.

```python
import jax
import jax.numpy as jnp
from jax import lax

FEAT = 8192
EXAMPLES = 6144


def draw_features(key, part):
    key = jax.random.fold_in(key, 11)
    keys = jax.random.split(key, 5)
    cluster_count = 16
    labels = jax.random.randint(keys[0], (EXAMPLES,), 0, cluster_count)
    row_scale = jnp.exp(jax.random.uniform(keys[1], (EXAMPLES,), jnp.float32, 0.0, 2.302585))
    col_scale = jnp.exp(jax.random.uniform(keys[2], (FEAT,), jnp.float32, 0.0, 2.302585))
    shared = jnp.clip(jax.random.normal(keys[3], (cluster_count, FEAT), jnp.float32), -5.0, 5.0)
    noise = jnp.clip(jax.random.normal(keys[4], (EXAMPLES, FEAT), jnp.float32), -5.0, 5.0)
    mixed = noise + 0.8 * shared[labels]
    values = 0.1 * row_scale[:, None] * col_scale[None, :] * mixed
    return values.astype(jnp.bfloat16)


def setup_inputs(seed: int = 0) -> dict:
    seeds = jax.random.split(jax.random.key(seed), 2)
    features = draw_features(jax.random.fold_in(seeds[1], 71), 0)
    return dict(features=features)


def reference(features):
    values = features.astype(jnp.float32)
    gram = jnp.dot(values, values.T, precision=lax.Precision.HIGHEST, preferred_element_type=jnp.float32)
    squares = lax.optimization_barrier(jnp.sum(values * values, axis=1)) + 1e-06
    scale = lax.rsqrt(squares)
    return gram * scale[:, None] * scale[None, :]
```

```python
import jax
import jax.numpy as jnp
from jax import lax
from jax.experimental import pallas as pl
from jax.experimental.pallas import tpu as pltpu
from jax.sharding import Mesh, PartitionSpec as P

AXES = ("xh", "z", "co", "yh", "yl", "xl")
SIZES = (2, 16, 2, 2, 2, 2)
ROWS = 96
DEPTH = 1024
PLANES = 16
GROUP = 4
EPS = 1e-06


def wide(left, right):
    return lax.dot_general(left, right, (((1,), (1,)), ((), ())), preferred_element_type=jnp.float32)


def squares_along_lanes(block):
    ones = jnp.ones((8, block.shape[1]), jnp.bfloat16)
    full = block.astype(jnp.float32)
    full = full * full
    high = full.astype(jnp.bfloat16)
    low = (full - high.astype(jnp.float32)).astype(jnp.bfloat16)
    return wide(ones, high) + wide(ones, low)


def partial_kernel(where_ref, *refs):
    rows_in, cols_in = refs[:4], refs[4 : 4 + PLANES]
    out_ref, rows_ref, cols_ref, sems = refs[4 + PLANES :]
    copies = []
    for i, source in enumerate(rows_in):
        at = pl.multiple_of(where_ref[i] * ROWS, ROWS)
        copies.append(pltpu.make_async_copy(source, rows_ref.at[pl.ds(at, ROWS)], sems.at[i]))
    for i, source in enumerate(cols_in):
        at = pl.multiple_of(where_ref[4 + i] * ROWS, ROWS)
        copies.append(pltpu.make_async_copy(source, cols_ref.at[pl.ds(at, ROWS)], sems.at[4 + i]))
    for copy in copies:
        copy.start()
    for copy in copies:
        copy.wait()
    width = GROUP * ROWS
    row_squares = squares_along_lanes(rows_ref[...])
    for group in range(PLANES // GROUP):
        block = cols_ref[group * width : (group + 1) * width]
        gram = wide(rows_ref[...], block)
        col_squares = squares_along_lanes(block)
        for row in range(4):
            slot = row * (PLANES // GROUP) + group
            out_ref[slot, 0:ROWS] = gram[row * ROWS : (row + 1) * ROWS]
            out_ref[slot, ROWS : ROWS + 4] = col_squares[0:4]
            out_ref[slot, ROWS + 4 : ROWS + 8, 0:ROWS] = row_squares[0:4, row * ROWS : (row + 1) * ROWS]


def final_kernel(parts_ref, out_ref):
    def total(core):
        terms = [parts_ref[(xh * 2 + core) * 4 + low] for xh in range(2) for low in range(4)]
        while len(terms) > 1:
            terms = [a + b for a, b in zip(terms[::2], terms[1::2])]
        return terms[0]

    halves = [total(0), total(1)]
    diagonal = lax.broadcasted_iota(jnp.int32, (ROWS, ROWS), 0) == lax.broadcasted_iota(jnp.int32, (ROWS, ROWS), 1)
    along = halves[0][ROWS + 4 : ROWS + 5, 0:ROWS]
    row_squares = jnp.sum(jnp.where(diagonal, along, 0.0), axis=1, keepdims=True)
    row_scale = lax.rsqrt(row_squares + EPS)
    scaled = [half[0:ROWS] * row_scale * lax.rsqrt(half[ROWS : ROWS + 1] + EPS) for half in halves]
    for low in range(GROUP):
        for core in range(2):
            at = (low * 2 + core) * ROWS
            out_ref[:, at : at + ROWS] = scaled[core][:, low * ROWS : (low + 1) * ROWS]


def shards(features):
    xh_yh = [(a, b) for a in range(2) for b in range(2)]
    own = lax.ppermute(features, ("xh", "yh"), [(2 * a + b, 2 * b + a) for a, b in xh_yh])
    upward = [(i, (i + 1) % PLANES) for i in range(PLANES)]
    downward = [(i, (i - 1) % PLANES) for i in range(PLANES)]
    blocks = {0: own}
    up = down = own
    for step in range(1, PLANES // 2 + 1):
        up = lax.ppermute(up, "z", upward)
        blocks[PLANES - step] = up
        if step < PLANES // 2:
            down = lax.ppermute(down, "z", downward)
            blocks[step] = down
    other = lax.ppermute(features, ("xh", "yh"), [(2 * a + b, 2 * b + 1 - a) for a, b in xh_yh])
    swap = [(0, 1), (1, 0)]
    own_across = lax.ppermute(own, "co", swap)
    other_across = lax.ppermute(other, "co", swap)
    yh, co, z = (lax.axis_index(name) for name in ("yh", "co", "z"))
    row_at = [2 * yh + co, 2 * (1 - yh) + co, 2 * yh + 1 - co, 2 * (1 - yh) + 1 - co]
    col_at = [(z + i) % PLANES for i in range(PLANES)]
    where = jnp.stack(row_at + col_at).astype(jnp.int32)
    groups = PLANES // GROUP
    parts = pl.pallas_call(
        partial_kernel,
        out_shape=jax.ShapeDtypeStruct((4 * groups, ROWS + 8, GROUP * ROWS), jnp.float32),
        in_specs=[pl.BlockSpec(memory_space=pltpu.SMEM)] + [pl.BlockSpec(memory_space=pl.ANY)] * (4 + PLANES),
        out_specs=pl.BlockSpec(memory_space=pltpu.VMEM),
        scratch_shapes=[
            pltpu.VMEM((4 * ROWS, DEPTH), jnp.bfloat16),
            pltpu.VMEM((PLANES * ROWS, DEPTH), jnp.bfloat16),
            pltpu.SemaphoreType.DMA((4 + PLANES,)),
        ],
        compiler_params=pltpu.CompilerParams(vmem_limit_bytes=40 << 20),
    )(where, own, other, own_across, other_across, *[blocks[i] for i in range(PLANES)])
    parts = lax.all_to_all(parts, ("xh", "co", "yl", "xl"), 0, 0)
    return pl.pallas_call(
        final_kernel,
        out_shape=jax.ShapeDtypeStruct((ROWS, 2 * GROUP * ROWS), jnp.float32),
        in_specs=[pl.BlockSpec(memory_space=pltpu.VMEM)],
        out_specs=pl.BlockSpec(memory_space=pltpu.VMEM),
        compiler_params=pltpu.CompilerParams(vmem_limit_bytes=40 << 20),
    )(parts)


def solution(mesh):
    split = Mesh(mesh.devices.reshape(SIZES), AXES)
    placed = P(("xh", "z", "co"), ("yh", "yl", "xl"))
    return jax.shard_map(shards, mesh=split, in_specs=(placed,), out_specs=placed, check_vma=False)
```

```python
import jax
import jax.numpy as jnp
from jax import lax
from jax.experimental import pallas as pl
from jax.experimental.pallas import tpu as pltpu
from jax.sharding import Mesh, PartitionSpec as P

AXES = ("xh", "z", "co", "yh", "yl", "xl")
SIZES = (2, 16, 2, 2, 2, 2)
ROWS = 96
TALL = 112
DEPTH = 1024
PLANES = 16
GROUP = 4
EPS = 1e-06
LANES = 128
TOP = 16384.0
FIRST_EXPONENT = 7
NORM_UNIT = 32.0
LIFT = 16384.0


def wide(left, right):
    return lax.dot_general(left, right, (((1,), (1,)), ((), ())), preferred_element_type=jnp.float32)


def on_diagonal(rows, lanes):
    return lax.broadcasted_iota(jnp.int32, (rows, lanes), 0) == lax.broadcasted_iota(jnp.int32, (rows, lanes), 1)


def scale_kernel(x_ref, out_ref):
    values = x_ref[...].astype(jnp.float32)
    largest = jnp.max(jnp.max(jnp.abs(values), axis=1, keepdims=True), axis=0, keepdims=True)
    scale = jnp.full((1, 1), 2.0**FIRST_EXPONENT, jnp.float32)
    exponent = jnp.full((1, 1), float(FIRST_EXPONENT), jnp.float32)
    for bit in (32, 16, 8, 4, 2, 1):
        fits = largest * scale * 2.0**bit < TOP
        scale = jnp.where(fits, scale * 2.0**bit, scale)
        exponent = jnp.where(fits, exponent + bit, exponent)
    scaled = values * scale
    out_ref[0:ROWS] = scaled.astype(jnp.bfloat16)
    norms = jnp.sqrt(jnp.sum(scaled * scaled, axis=1, keepdims=True)) * (1.0 / NORM_UNIT)
    along = jnp.sum(jnp.where(on_diagonal(ROWS, LANES), norms, 0.0), axis=0, keepdims=True)

    def rounded(x):
        return x.astype(jnp.bfloat16).astype(jnp.float32)

    high = rounded(along)
    middle = rounded((along - high) * 256.0)
    low = rounded((along - high - middle * (1.0 / 256.0)) * 65536.0)
    row = lax.broadcasted_iota(jnp.int32, (TALL - ROWS, LANES), 0)
    info = jnp.where(row == 0, high, jnp.where(row == 1, middle, jnp.where(row == 2, low, exponent)))
    out_ref[ROWS:TALL] = jnp.zeros((TALL - ROWS, DEPTH), jnp.bfloat16)
    out_ref[ROWS:TALL, 0:LANES] = jnp.where(row < 4, info, 0.0).astype(jnp.bfloat16)


def norm_of(info):
    return (info[0:1] + info[1:2] * (1.0 / 256.0) + info[2:3] * (1.0 / 65536.0)) * NORM_UNIT


def inverse(norm):
    return jnp.where(norm > 0.0, 1.0 / jnp.where(norm > 0.0, norm, 1.0), 0.0)


def partial_kernel(where_ref, *refs):
    rows_in, cols_ref = refs[:4], refs[4]
    out_ref, rows_ref, scale_ref, info_ref = refs[5:]
    groups = PLANES // GROUP
    width = GROUP * ROWS
    diagonal = on_diagonal(ROWS, LANES)
    for i, source in enumerate(rows_in):
        at = pl.multiple_of(where_ref[i] * ROWS, ROWS)
        rows_ref[pl.ds(at, ROWS)] = source[0:ROWS]
        info = source[ROWS:TALL, 0:LANES].astype(jnp.float32)
        down = jnp.sum(jnp.where(diagonal, inverse(norm_of(info)) * LIFT, 0.0), axis=1, keepdims=True)
        scale_ref[pl.ds(at, ROWS)] = jnp.broadcast_to(down, (ROWS, LANES))
        for group in range(groups):
            out_ref[where_ref[i] * groups + group, ROWS + 4 : ROWS + 8, 0:LANES] = info[0:4]
    for group in range(groups):
        for low in range(GROUP):
            start = (group * GROUP + low) * TALL
            info = cols_ref[start + ROWS : start + TALL, 0:LANES].astype(jnp.float32)
            info_ref[0:4, low * ROWS : (low + 1) * ROWS] = info[0:4, 0:ROWS]
        starts = [(group * GROUP + low) * TALL for low in range(GROUP)]
        block = jnp.concatenate([cols_ref[start : start + ROWS] for start in starts], axis=0)
        info = info_ref[0:4]
        across = inverse(norm_of(info))
        gram = wide(rows_ref[...], block)
        for row in range(4):
            slot = row * groups + group
            down = scale_ref[row * ROWS : (row + 1) * ROWS, 0:1]
            out_ref[slot, 0:ROWS] = gram[row * ROWS : (row + 1) * ROWS] * down * across
            out_ref[slot, ROWS : ROWS + 4] = info


def final_kernel(parts_ref, out_ref):
    diagonal = on_diagonal(ROWS, LANES)
    slots = [[(xh * 2 + core) * 4 + low for xh in range(2) for low in range(4)] for core in range(2)]

    def true_norms(core, first, lanes):
        infos = [parts_ref[slot, first : first + 4, 0:lanes] for slot in slots[core]]
        return [norm_of(info) * jnp.exp2(-info[3:4]) for info in infos]

    def weights(norms):
        total = norms[0] * norms[0]
        for norm in norms[1:]:
            total += norm * norm
        shrink = lax.rsqrt(total + EPS) * LIFT**-0.5
        return [norm * shrink for norm in norms]

    rows = weights(true_norms(0, ROWS + 4, LANES))
    rows = [jnp.sum(jnp.where(diagonal, along, 0.0), axis=1, keepdims=True) for along in rows]
    for core in range(2):
        cols = weights(true_norms(core, ROWS, GROUP * ROWS))
        total = jnp.zeros((ROWS, GROUP * ROWS), jnp.float32)
        for slot, down, across in zip(slots[core], rows, cols):
            total += parts_ref[slot, 0:ROWS] * down * across
        for low in range(GROUP):
            at = (low * 2 + core) * ROWS
            out_ref[:, at : at + ROWS] = total[:, low * ROWS : (low + 1) * ROWS]


def shards(features):
    in_vmem = pl.BlockSpec(memory_space=pltpu.VMEM)
    params = pltpu.CompilerParams(vmem_limit_bytes=40 << 20)
    scaled = pl.pallas_call(
        scale_kernel,
        out_shape=jax.ShapeDtypeStruct((TALL, DEPTH), jnp.bfloat16),
        in_specs=[in_vmem],
        out_specs=in_vmem,
        compiler_params=params,
    )(features)
    pairs = [(a, b) for a in range(2) for b in range(2)]
    to_own = [(2 * a + b, 2 * b + a) for a, b in pairs]
    to_other = [(2 * a + b, 2 * b + 1 - a) for a, b in pairs]
    own = lax.ppermute(scaled, ("xh", "yh"), to_own)
    across = lax.ppermute(scaled, "co", [(0, 1), (1, 0)])
    other = lax.ppermute(scaled, ("xh", "yh"), to_other)
    own_across = lax.ppermute(across, ("xh", "yh"), to_own)
    other_across = lax.ppermute(across, ("xh", "yh"), to_other)
    columns = lax.all_gather(own.astype(jnp.float16), "z", axis=0, tiled=True).astype(jnp.bfloat16)
    yh, co = lax.axis_index("yh"), lax.axis_index("co")
    where = jnp.stack([2 * yh + co, 2 * (1 - yh) + co, 2 * yh + 1 - co, 2 * (1 - yh) + 1 - co]).astype(jnp.int32)
    groups = PLANES // GROUP
    parts = pl.pallas_call(
        partial_kernel,
        out_shape=jax.ShapeDtypeStruct((4 * groups, ROWS + 8, GROUP * ROWS), jnp.float32),
        in_specs=[pl.BlockSpec(memory_space=pltpu.SMEM)] + [in_vmem] * 5,
        out_specs=in_vmem,
        scratch_shapes=[
            pltpu.VMEM((4 * ROWS, DEPTH), jnp.bfloat16),
            pltpu.VMEM((4 * ROWS, LANES), jnp.float32),
            pltpu.VMEM((8, GROUP * ROWS), jnp.float32),
        ],
        compiler_params=params,
    )(where, own, other, own_across, other_across, columns)
    parts = lax.all_to_all(parts.astype(jnp.float16), ("xh", "co", "yl", "xl"), 0, 0)
    return pl.pallas_call(
        final_kernel,
        out_shape=jax.ShapeDtypeStruct((ROWS, 2 * GROUP * ROWS), jnp.float32),
        in_specs=[in_vmem],
        out_specs=in_vmem,
        compiler_params=params,
    )(parts.astype(jnp.float32))


def solution(mesh):
    split = Mesh(mesh.devices.reshape(SIZES), AXES)
    placed = P(("xh", "z", "co"), ("yh", "yl", "xl"))
    return jax.shard_map(shards, mesh=split, in_specs=(placed,), out_specs=placed, check_vma=False)
```

```python
import itertools

import jax
import jax.numpy as jnp
from jax import lax
from jax.experimental import pallas as pl
from jax.experimental.pallas import tpu as pltpu
from jax.sharding import Mesh, PartitionSpec as P

AXES = ("xh", "z", "co", "yh", "yl", "xl")
SIZES = (2, 16, 2, 2, 2, 2)
ROWS = 96
TALL = 112
DEPTH = 1024
PLANES = 16
GROUP = 4
EPS = 1e-06
LANES = 128
TOP = 16384.0
FIRST_EXPONENT = 7
NORM_UNIT = 32.0
LIFT = 16384.0


def wide(left, right):
    return lax.dot_general(left, right, (((1,), (1,)), ((), ())), preferred_element_type=jnp.float32)


def on_diagonal(rows, lanes):
    return lax.broadcasted_iota(jnp.int32, (rows, lanes), 0) == lax.broadcasted_iota(jnp.int32, (rows, lanes), 1)


def scale_kernel(x_ref, out_ref):
    values = x_ref[...].astype(jnp.float32)
    largest = jnp.max(jnp.max(jnp.abs(values), axis=1, keepdims=True), axis=0, keepdims=True)
    scale = jnp.full((1, 1), 2.0**FIRST_EXPONENT, jnp.float32)
    exponent = jnp.full((1, 1), float(FIRST_EXPONENT), jnp.float32)
    for bit in (32, 16, 8, 4, 2, 1):
        fits = largest * scale * 2.0**bit < TOP
        scale = jnp.where(fits, scale * 2.0**bit, scale)
        exponent = jnp.where(fits, exponent + bit, exponent)
    scaled = values * scale
    out_ref[0:ROWS] = scaled.astype(jnp.bfloat16)
    norms = jnp.sqrt(jnp.sum(scaled * scaled, axis=1, keepdims=True)) * (1.0 / NORM_UNIT)
    along = jnp.sum(jnp.where(on_diagonal(ROWS, LANES), norms, 0.0), axis=0, keepdims=True)

    def rounded(x):
        return x.astype(jnp.bfloat16).astype(jnp.float32)

    high = rounded(along)
    middle = rounded((along - high) * 256.0)
    low = rounded((along - high - middle * (1.0 / 256.0)) * 65536.0)
    row = lax.broadcasted_iota(jnp.int32, (TALL - ROWS, LANES), 0)
    info = jnp.where(row == 0, high, jnp.where(row == 1, middle, jnp.where(row == 2, low, exponent)))
    out_ref[ROWS:TALL] = jnp.zeros((TALL - ROWS, DEPTH), jnp.bfloat16)
    out_ref[ROWS:TALL, 0:LANES] = jnp.where(row < 4, info, 0.0).astype(jnp.bfloat16)


def norm_of(info):
    return (info[0:1] + info[1:2] * (1.0 / 256.0) + info[2:3] * (1.0 / 65536.0)) * NORM_UNIT


def inverse(norm):
    return jnp.where(norm > 0.0, 1.0 / jnp.where(norm > 0.0, norm, 1.0), 0.0)


def partial_kernel(where_ref, *refs):
    rows_in, cols_ref = refs[:4], refs[4]
    out_ref, rows_ref, scale_ref, info_ref = refs[5:]
    groups = PLANES // GROUP
    width = GROUP * ROWS
    diagonal = on_diagonal(ROWS, LANES)
    for i, source in enumerate(rows_in):
        at = pl.multiple_of(where_ref[i] * ROWS, ROWS)
        rows_ref[pl.ds(at, ROWS)] = source[0:ROWS]
        info = source[ROWS:TALL, 0:LANES].astype(jnp.float32)
        down = jnp.sum(jnp.where(diagonal, inverse(norm_of(info)) * LIFT, 0.0), axis=1, keepdims=True)
        scale_ref[pl.ds(at, ROWS)] = jnp.broadcast_to(down, (ROWS, LANES))
        for group in range(groups):
            out_ref[where_ref[i] * groups + group, ROWS + 4 : ROWS + 8, 0:LANES] = info[0:4]
    for group in range(groups):
        for low in range(GROUP):
            start = (group * GROUP + low) * TALL
            info = cols_ref[start + ROWS : start + TALL, 0:LANES].astype(jnp.float32)
            info_ref[0:4, low * ROWS : (low + 1) * ROWS] = info[0:4, 0:ROWS]
        starts = [(group * GROUP + low) * TALL for low in range(GROUP)]
        block = jnp.concatenate([cols_ref[start : start + ROWS] for start in starts], axis=0)
        info = info_ref[0:4]
        across = inverse(norm_of(info))
        gram = wide(rows_ref[...], block)
        for row in range(4):
            slot = row * groups + group
            down = scale_ref[row * ROWS : (row + 1) * ROWS, 0:1]
            out_ref[slot, 0:ROWS] = gram[row * ROWS : (row + 1) * ROWS] * down * across
            out_ref[slot, ROWS : ROWS + 4] = info


def final_kernel(parts_ref, out_ref):
    diagonal = on_diagonal(ROWS, LANES)
    slots = [[(xh * 2 + core) * 4 + low for xh in range(2) for low in range(4)] for core in range(2)]

    def true_norms(core, first, lanes):
        infos = [parts_ref[slot, first : first + 4, 0:lanes] for slot in slots[core]]
        return [norm_of(info) * jnp.exp2(-info[3:4]) for info in infos]

    def weights(norms):
        total = norms[0] * norms[0]
        for norm in norms[1:]:
            total += norm * norm
        shrink = lax.rsqrt(total + EPS) * LIFT**-0.5
        return [norm * shrink for norm in norms]

    rows = weights(true_norms(0, ROWS + 4, LANES))
    rows = [jnp.sum(jnp.where(diagonal, along, 0.0), axis=1, keepdims=True) for along in rows]
    for core in range(2):
        cols = weights(true_norms(core, ROWS, GROUP * ROWS))
        total = jnp.zeros((ROWS, GROUP * ROWS), jnp.float32)
        for slot, down, across in zip(slots[core], rows, cols):
            total += parts_ref[slot, 0:ROWS] * down * across
        for low in range(GROUP):
            at = (low * 2 + core) * ROWS
            out_ref[:, at : at + ROWS] = total[:, low * ROWS : (low + 1) * ROWS]


def shards(features):
    in_vmem = pl.BlockSpec(memory_space=pltpu.VMEM)
    params = pltpu.CompilerParams(vmem_limit_bytes=40 << 20)
    scaled = pl.pallas_call(
        scale_kernel,
        out_shape=jax.ShapeDtypeStruct((TALL, DEPTH), jnp.bfloat16),
        in_specs=[in_vmem],
        out_specs=in_vmem,
        compiler_params=params,
    )(features)
    def moved(own, across):
        pairs = []
        for a, c, b in itertools.product(range(2), repeat=3):
            to = ({(0, 0): (1, 0), (0, 1): (0, 0), (1, 1): (0, 1), (1, 0): (1, 1)} if own else {(a, b): (1 - b, 1 - a)})[a, b]
            pairs.append(((a * 2 + c) * 2 + b, (to[0] * 2 + (c ^ across)) * 2 + to[1]))
        return lax.ppermute(scaled, ("xh", "co", "yh"), pairs)

    own, own_across, other, other_across = moved(1, 0), moved(1, 1), moved(0, 0), moved(0, 1)
    columns = lax.all_gather(own.astype(jnp.float16), "z", axis=0, tiled=True).astype(jnp.bfloat16)
    yh, co = lax.axis_index("yh"), lax.axis_index("co")
    where = jnp.stack([2 * yh + co, 2 * (1 - yh) + co, 2 * yh + 1 - co, 2 * (1 - yh) + 1 - co]).astype(jnp.int32)
    groups = PLANES // GROUP
    parts = pl.pallas_call(
        partial_kernel,
        out_shape=jax.ShapeDtypeStruct((4 * groups, ROWS + 8, GROUP * ROWS), jnp.float32),
        in_specs=[pl.BlockSpec(memory_space=pltpu.SMEM)] + [in_vmem] * 5,
        out_specs=in_vmem,
        scratch_shapes=[
            pltpu.VMEM((4 * ROWS, DEPTH), jnp.bfloat16),
            pltpu.VMEM((4 * ROWS, LANES), jnp.float32),
            pltpu.VMEM((8, GROUP * ROWS), jnp.float32),
        ],
        compiler_params=params,
    )(where, own, other, own_across, other_across, columns)
    parts = lax.all_to_all(parts.astype(jnp.float16), ("xh", "co", "yl", "xl"), 0, 0)
    return pl.pallas_call(
        final_kernel,
        out_shape=jax.ShapeDtypeStruct((ROWS, 2 * GROUP * ROWS), jnp.float32),
        in_specs=[in_vmem],
        out_specs=in_vmem,
        compiler_params=params,
    )(parts.astype(jnp.float32))


def solution(mesh):
    split = Mesh(mesh.devices.reshape(SIZES), AXES)
    placed = P(("xh", "z", "co"), ("yh", "yl", "xl"))
    return jax.shard_map(shards, mesh=split, in_specs=(placed,), out_specs=placed, check_vma=False)
```

```python
import jax
import jax.numpy as jnp
from jax import lax
from jax.experimental import pallas as pl
from jax.experimental.pallas import tpu as pltpu
from jax.sharding import Mesh, PartitionSpec as P

AXES = ("xh", "z", "co", "yh", "yl", "xl")
SIZES = (2, 16, 2, 2, 2, 2)
ROWS = 96
HALF = 48
INFO = 16
DEPTH = 1024
PLANES = 16
GROUP = 4
GROUPS = PLANES // GROUP
WIDTH = GROUP * HALF
EPS = 1e-06
LANES = 128
TOP = 16384.0
FIRST_EXPONENT = 7
NORM_UNIT = 32.0
LIFT = 16384.0


def wide(left, right):
    return lax.dot_general(left, right, (((1,), (1,)), ((), ())), preferred_element_type=jnp.float32)


def on_diagonal(rows, lanes, shift=0):
    row = lax.broadcasted_iota(jnp.int32, (rows, lanes), 0)
    return row + shift == lax.broadcasted_iota(jnp.int32, (rows, lanes), 1)


def rounded(x):
    return x.astype(jnp.bfloat16).astype(jnp.float32)


def three_parts(along):
    high = rounded(along)
    middle = rounded((along - high) * 256.0)
    low = rounded((along - high - middle * (1.0 / 256.0)) * 65536.0)
    return high, middle, low


def stacked(parts, rows, lanes):
    row = lax.broadcasted_iota(jnp.int32, (rows, lanes), 0)
    out = jnp.zeros((rows, lanes), jnp.float32)
    for i, part in enumerate(parts):
        out = jnp.where(row == i, part, out)
    return out


def exponent_for(largest):
    scale = jnp.full(largest.shape, 2.0**FIRST_EXPONENT, jnp.float32)
    exponent = jnp.full(largest.shape, float(FIRST_EXPONENT), jnp.float32)
    for bit in (32, 16, 8, 4, 2, 1):
        fits = largest * scale * 2.0**bit < TOP
        scale = jnp.where(fits, scale * 2.0**bit, scale)
        exponent = jnp.where(fits, exponent + bit, exponent)
    return scale, exponent


def scale_kernel(yh_ref, x_ref, first_ref, second_ref):
    values = x_ref[...].astype(jnp.float32)
    largest = jnp.max(jnp.max(jnp.abs(values), axis=1, keepdims=True), axis=0, keepdims=True)
    scale, exponent = exponent_for(largest)
    scaled = values * scale
    norms = jnp.sqrt(jnp.sum(scaled * scaled, axis=1, keepdims=True)) * (1.0 / NORM_UNIT)
    infos = []
    for half in range(2):
        at = half * HALF
        along = jnp.sum(
            jnp.where(on_diagonal(HALF, LANES), norms[at : at + HALF], 0.0), axis=0, keepdims=True
        )
        infos.append(stacked((*three_parts(along), exponent), INFO, LANES))
    whole = scaled.astype(jnp.bfloat16)
    flipped = yh_ref[0] == 1

    def fill(ref, half):
        ref[0:HALF] = whole[half * HALF : (half + 1) * HALF]
        ref[HALF : HALF + INFO] = jnp.zeros((INFO, DEPTH), jnp.bfloat16)
        ref[HALF : HALF + INFO, 0:LANES] = infos[half].astype(jnp.bfloat16)

    @pl.when(jnp.logical_not(flipped))
    def _():
        fill(first_ref, 0)
        fill(second_ref, 1)

    @pl.when(flipped)
    def _():
        fill(first_ref, 1)
        fill(second_ref, 0)


def scaled_norm(info):
    return (info[0:1] + info[1:2] * (1.0 / 256.0) + info[2:3] * (1.0 / 65536.0)) * NORM_UNIT


def inverse(norm):
    return jnp.where(norm > 0.0, 1.0 / jnp.where(norm > 0.0, norm, 1.0), 0.0)


def encoded(norm):
    scale, exponent = exponent_for(norm * (1.0 / NORM_UNIT))
    return (*three_parts(norm * scale * (1.0 / NORM_UNIT)), exponent)


def partial_kernel(xh_ref, rows_ref, cols_ref, info_ref, out_ref, left_ref, lanes_ref):
    xh = xh_ref[0]
    squares = []
    for row in range(4):
        both = []
        for i, yh in enumerate((xh, 1 - xh)):
            block = rows_ref[2 * row + yh]
            left_ref[i, row * ROWS : (row + 1) * ROWS] = block
            full = block.astype(jnp.float32)
            both.append(jnp.sum(full * full, axis=1, keepdims=True))
        squares.append(both[0] + both[1])
    for z in range(PLANES):
        lanes_ref[0:8, z * HALF : (z + 1) * HALF] = info_ref[z, 0:8, 0:HALF]
    gram, col_squares = None, None
    for i in range(2):
        block = jnp.concatenate([cols_ref[z, i * HALF : (i + 1) * HALF] for z in range(PLANES)], axis=0)
        info = lanes_ref[4 * i : 4 * i + 4]
        back = jnp.exp2(-info[3:4])
        norm = scaled_norm(info) * back
        product = wide(left_ref[i], block) * back
        gram = product if gram is None else gram + product
        col_squares = norm * norm if col_squares is None else col_squares + norm * norm
    col_norms = jnp.sqrt(col_squares)
    gram = gram * (inverse(col_norms) * LIFT)
    col_info = stacked(encoded(col_norms), 4, PLANES * HALF)
    for row in range(4):
        row_norms = jnp.sqrt(squares[row])
        scaled = gram[row * ROWS : (row + 1) * ROWS] * inverse(row_norms)
        along = jnp.sum(jnp.where(on_diagonal(ROWS, LANES), row_norms, 0.0), axis=0, keepdims=True)
        row_info = stacked(encoded(along), 4, LANES)
        for group in range(GROUPS):
            slot = row * GROUPS + group
            at = group * WIDTH
            for half in range(2):
                lanes = slice(half * WIDTH, (half + 1) * WIDTH)
                out_ref[slot, 0:HALF, lanes] = scaled[half * HALF : (half + 1) * HALF, at : at + WIDTH]
                out_ref[slot, HALF : HALF + 4, lanes] = col_info[:, at : at + WIDTH]
            out_ref[slot, HALF + 4 : HALF + 8, 0:LANES] = row_info


def final_kernel(parts_ref, out_ref):
    left = lax.broadcasted_iota(jnp.int32, (HALF, 2 * WIDTH), 1) < WIDTH

    def weights(slots, first, lanes):
        infos = [parts_ref[slot, first : first + 4, 0:lanes] for slot in slots]
        norms = [scaled_norm(info) * jnp.exp2(-info[3:4]) for info in infos]
        total = norms[0] * norms[0]
        for norm in norms[1:]:
            total += norm * norm
        shrink = lax.rsqrt(total + EPS) * LIFT**-0.5
        return [norm * shrink for norm in norms]

    downs = []
    for along in weights(range(4), HALF + 4, LANES):
        top, bottom = [
            jnp.sum(jnp.where(on_diagonal(HALF, LANES, at), along, 0.0), axis=1, keepdims=True) for at in (0, HALF)
        ]
        downs.append(jnp.where(left, top, bottom))
    for xh in range(2):
        for core in range(2):
            slots = [(xh * 2 + core) * 4 + low for low in range(4)]
            total = None
            for slot, down, across in zip(slots, downs, weights(slots, HALF, 2 * WIDTH)):
                term = parts_ref[slot, 0:HALF] * down * across
                total = term if total is None else total + term
            for low in range(GROUP):
                at = (low * 2 + core) * ROWS + xh * HALF
                for half in range(2):
                    source = half * WIDTH + low * HALF
                    out_ref[half * HALF : (half + 1) * HALF, at : at + HALF] = total[:, source : source + HALF]


def shards(features):
    in_vmem = pl.BlockSpec(memory_space=pltpu.VMEM)
    in_smem = pl.BlockSpec(memory_space=pltpu.SMEM)
    params = pltpu.CompilerParams(vmem_limit_bytes=40 << 20)
    xh, yh = (lax.axis_index(name).astype(jnp.int32).reshape(1) for name in ("xh", "yh"))
    half_block = jax.ShapeDtypeStruct((HALF + INFO, DEPTH), jnp.bfloat16)
    first, second = pl.pallas_call(
        scale_kernel,
        out_shape=(half_block, half_block),
        in_specs=[in_smem, in_vmem],
        out_specs=(in_vmem, in_vmem),
        compiler_params=params,
    )(yh, features)
    pairs = [(a, b) for a in range(2) for b in range(2)]
    first = lax.ppermute(first, ("xh", "yh"), [(2 * a + b, 2 * b + a) for a, b in pairs])
    second = lax.ppermute(second, ("xh", "yh"), [(2 * a + b, 2 * (1 - b) + a) for a, b in pairs])
    rows = lax.all_to_all(jnp.broadcast_to(features, (8, ROWS, DEPTH)), ("xh", "co", "yh"), 0, 0)
    block = jnp.concatenate([first[:HALF], second[:HALF], first[HALF : HALF + 4], second[HALF : HALF + 4]], axis=0)
    columns = lax.all_gather(block.astype(jnp.float16), "z", axis=0, tiled=False)
    info = columns[:, ROWS:, :LANES].astype(jnp.float32)
    parts = pl.pallas_call(
        partial_kernel,
        out_shape=jax.ShapeDtypeStruct((4 * GROUPS, HALF + 8, 2 * WIDTH), jnp.float32),
        in_specs=[in_smem] + [in_vmem] * 3,
        out_specs=in_vmem,
        scratch_shapes=[
            pltpu.VMEM((2, 4 * ROWS, DEPTH), jnp.bfloat16),
            pltpu.VMEM((8, PLANES * HALF), jnp.float32),
        ],
        compiler_params=params,
    )(xh, rows, columns.astype(jnp.bfloat16), info)
    parts = lax.all_to_all(parts.astype(jnp.float16), ("xh", "co", "yl", "xl"), 0, 0)
    return pl.pallas_call(
        final_kernel,
        out_shape=jax.ShapeDtypeStruct((ROWS, 4 * WIDTH), jnp.float32),
        in_specs=[in_vmem],
        out_specs=in_vmem,
        compiler_params=params,
    )(parts.astype(jnp.float32))


def solution(mesh):
    split = Mesh(mesh.devices.reshape(SIZES), AXES)
    placed = P(("xh", "z", "co"), ("yh", "yl", "xl"))
    return jax.shard_map(shards, mesh=split, in_specs=(placed,), out_specs=placed, check_vma=False)
```

```python
import itertools

import jax
import jax.numpy as jnp
from jax import lax
from jax.experimental import pallas as pl
from jax.experimental.pallas import tpu as pltpu
from jax.sharding import Mesh, PartitionSpec as P

AXES = ("xh", "z", "co", "yh", "yl", "xl")
SIZES = (2, 16, 2, 2, 2, 2)
ROWS = 96
HALF = 48
INFO = 16
DEPTH = 1024
PLANES = 16
GROUP = 4
GROUPS = PLANES // GROUP
WIDTH = GROUP * HALF
EPS = 1e-06
LANES = 128
TOP = 16384.0
FIRST_EXPONENT = 7
NORM_UNIT = 32.0
LIFT = 16384.0


def wide(left, right):
    return lax.dot_general(left, right, (((1,), (1,)), ((), ())), preferred_element_type=jnp.float32)


def on_diagonal(rows, lanes, shift=0):
    row = lax.broadcasted_iota(jnp.int32, (rows, lanes), 0)
    return row + shift == lax.broadcasted_iota(jnp.int32, (rows, lanes), 1)


def rounded(x):
    return x.astype(jnp.bfloat16).astype(jnp.float32)


def three_parts(along):
    high = rounded(along)
    middle = rounded((along - high) * 256.0)
    low = rounded((along - high - middle * (1.0 / 256.0)) * 65536.0)
    return high, middle, low


def stacked(parts, rows, lanes):
    row = lax.broadcasted_iota(jnp.int32, (rows, lanes), 0)
    out = jnp.zeros((rows, lanes), jnp.float32)
    for i, part in enumerate(parts):
        out = jnp.where(row == i, part, out)
    return out


def exponent_for(largest):
    scale = jnp.full(largest.shape, 2.0**FIRST_EXPONENT, jnp.float32)
    exponent = jnp.full(largest.shape, float(FIRST_EXPONENT), jnp.float32)
    for bit in (32, 16, 8, 4, 2, 1):
        fits = largest * scale * 2.0**bit < TOP
        scale = jnp.where(fits, scale * 2.0**bit, scale)
        exponent = jnp.where(fits, exponent + bit, exponent)
    return scale, exponent


def scale_kernel(yh_ref, x_ref, first_ref, second_ref):
    values = x_ref[...].astype(jnp.float32)
    largest = jnp.max(jnp.max(jnp.abs(values), axis=1, keepdims=True), axis=0, keepdims=True)
    scale, exponent = exponent_for(largest)
    scaled = values * scale
    norms = jnp.sqrt(jnp.sum(scaled * scaled, axis=1, keepdims=True)) * (1.0 / NORM_UNIT)
    infos = []
    for half in range(2):
        at = half * HALF
        along = jnp.sum(
            jnp.where(on_diagonal(HALF, LANES), norms[at : at + HALF], 0.0), axis=0, keepdims=True
        )
        infos.append(stacked((*three_parts(along), exponent), INFO, LANES))
    whole = scaled.astype(jnp.bfloat16)
    flipped = yh_ref[0] == 1

    def fill(ref, half):
        ref[0:HALF] = whole[half * HALF : (half + 1) * HALF]
        ref[HALF : HALF + INFO] = jnp.zeros((INFO, DEPTH), jnp.bfloat16)
        ref[HALF : HALF + INFO, 0:LANES] = infos[half].astype(jnp.bfloat16)

    @pl.when(jnp.logical_not(flipped))
    def _():
        fill(first_ref, 0)
        fill(second_ref, 1)

    @pl.when(flipped)
    def _():
        fill(first_ref, 1)
        fill(second_ref, 0)


def scaled_norm(info):
    return (info[0:1] + info[1:2] * (1.0 / 256.0) + info[2:3] * (1.0 / 65536.0)) * NORM_UNIT


def inverse(norm):
    return jnp.where(norm > 0.0, 1.0 / jnp.where(norm > 0.0, norm, 1.0), 0.0)


def encoded(norm):
    scale, exponent = exponent_for(norm * (1.0 / NORM_UNIT))
    return (*three_parts(norm * scale * (1.0 / NORM_UNIT)), exponent)


def partial_kernel(xh_ref, rows_ref, cols_ref, info_ref, out_ref, left_ref, lanes_ref):
    xh = xh_ref[0]
    squares = []
    for row in range(4):
        both = []
        for i, yh in enumerate((xh, 1 - xh)):
            block = rows_ref[2 * row + yh]
            left_ref[i, row * ROWS : (row + 1) * ROWS] = block
            full = block.astype(jnp.float32)
            both.append(jnp.sum(full * full, axis=1, keepdims=True))
        squares.append(both[0] + both[1])
    for z in range(PLANES):
        lanes_ref[0:8, z * HALF : (z + 1) * HALF] = info_ref[z, 0:8, 0:HALF]
    gram, col_squares = None, None
    for i in range(2):
        block = jnp.concatenate([cols_ref[z, i * HALF : (i + 1) * HALF] for z in range(PLANES)], axis=0)
        info = lanes_ref[4 * i : 4 * i + 4]
        back = jnp.exp2(-info[3:4])
        norm = scaled_norm(info) * back
        product = wide(left_ref[i], block) * back
        gram = product if gram is None else gram + product
        col_squares = norm * norm if col_squares is None else col_squares + norm * norm
    col_norms = jnp.sqrt(col_squares)
    gram = gram * (inverse(col_norms) * LIFT)
    col_info = stacked(encoded(col_norms), 4, PLANES * HALF)
    for row in range(4):
        row_norms = jnp.sqrt(squares[row])
        scaled = gram[row * ROWS : (row + 1) * ROWS] * inverse(row_norms)
        along = jnp.sum(jnp.where(on_diagonal(ROWS, LANES), row_norms, 0.0), axis=0, keepdims=True)
        row_info = stacked(encoded(along), 4, LANES)
        for group in range(GROUPS):
            slot = row * GROUPS + group
            at = group * WIDTH
            for half in range(2):
                lanes = slice(half * WIDTH, (half + 1) * WIDTH)
                out_ref[slot, 0:HALF, lanes] = scaled[half * HALF : (half + 1) * HALF, at : at + WIDTH]
                out_ref[slot, HALF : HALF + 4, lanes] = col_info[:, at : at + WIDTH]
            out_ref[slot, HALF + 4 : HALF + 8, 0:LANES] = row_info


def final_kernel(parts_ref, out_ref):
    left = lax.broadcasted_iota(jnp.int32, (HALF, 2 * WIDTH), 1) < WIDTH

    def weights(slots, first, lanes):
        infos = [parts_ref[slot, first : first + 4, 0:lanes] for slot in slots]
        norms = [scaled_norm(info) * jnp.exp2(-info[3:4]) for info in infos]
        total = norms[0] * norms[0]
        for norm in norms[1:]:
            total += norm * norm
        shrink = lax.rsqrt(total + EPS) * LIFT**-0.5
        return [norm * shrink for norm in norms]

    downs = []
    for along in weights(range(4), HALF + 4, LANES):
        top, bottom = [
            jnp.sum(jnp.where(on_diagonal(HALF, LANES, at), along, 0.0), axis=1, keepdims=True) for at in (0, HALF)
        ]
        downs.append(jnp.where(left, top, bottom))
    for xh in range(2):
        for core in range(2):
            slots = [(xh * 2 + core) * 4 + low for low in range(4)]
            total = None
            for slot, down, across in zip(slots, downs, weights(slots, HALF, 2 * WIDTH)):
                term = parts_ref[slot, 0:HALF] * down * across
                total = term if total is None else total + term
            for low in range(GROUP):
                at = (low * 2 + core) * ROWS + xh * HALF
                for half in range(2):
                    source = half * WIDTH + low * HALF
                    out_ref[half * HALF : (half + 1) * HALF, at : at + HALF] = total[:, source : source + HALF]


def shards(features):
    in_vmem = pl.BlockSpec(memory_space=pltpu.VMEM)
    in_smem = pl.BlockSpec(memory_space=pltpu.SMEM)
    params = pltpu.CompilerParams(vmem_limit_bytes=40 << 20)
    xh, yh = (lax.axis_index(name).astype(jnp.int32).reshape(1) for name in ("xh", "yh"))
    half_block = jax.ShapeDtypeStruct((HALF + INFO, DEPTH), jnp.bfloat16)
    first, second = pl.pallas_call(
        scale_kernel,
        out_shape=(half_block, half_block),
        in_specs=[in_smem, in_vmem],
        out_specs=(in_vmem, in_vmem),
        compiler_params=params,
    )(yh, features)
    firsts, seconds = [], []
    for a, b, yl in itertools.product(range(2), repeat=3):
        to = yl if a == b else 1 - yl
        firsts.append((4 * a + 2 * b + yl, 4 * b + 2 * a + to))
        seconds.append((4 * a + 2 * b + yl, 4 * (1 - b) + 2 * a + to))
    first = lax.ppermute(first, ("xh", "yh", "yl"), firsts)
    second = lax.ppermute(second, ("xh", "yh", "yl"), seconds)
    groups = [
        [8 * a + 4 * c + 2 * b + (b ^ mirror) for a, c, b in itertools.product(range(2), repeat=3)]
        for mirror in range(2)
    ]
    rows = lax.all_to_all(
        jnp.broadcast_to(features, (8, ROWS, DEPTH)), ("xh", "co", "yh", "yl"), 0, 0, axis_index_groups=groups
    )
    block = jnp.concatenate([first[:HALF], second[:HALF], first[HALF : HALF + 4], second[HALF : HALF + 4]], axis=0)
    columns = lax.all_gather(block.astype(jnp.float16), "z", axis=0, tiled=False)
    info = columns[:, ROWS:, :LANES].astype(jnp.float32)
    parts = pl.pallas_call(
        partial_kernel,
        out_shape=jax.ShapeDtypeStruct((4 * GROUPS, HALF + 8, 2 * WIDTH), jnp.float32),
        in_specs=[in_smem] + [in_vmem] * 3,
        out_specs=in_vmem,
        scratch_shapes=[
            pltpu.VMEM((2, 4 * ROWS, DEPTH), jnp.bfloat16),
            pltpu.VMEM((8, PLANES * HALF), jnp.float32),
        ],
        compiler_params=params,
    )(xh, rows, columns.astype(jnp.bfloat16), info)
    parts = lax.all_to_all(parts.astype(jnp.float16), ("xh", "co", "yl", "xl"), 0, 0)
    return pl.pallas_call(
        final_kernel,
        out_shape=jax.ShapeDtypeStruct((ROWS, 4 * WIDTH), jnp.float32),
        in_specs=[in_vmem],
        out_specs=in_vmem,
        compiler_params=params,
    )(parts.astype(jnp.float32))


def solution(mesh):
    split = Mesh(mesh.devices.reshape(SIZES), AXES)
    placed = P(("xh", "z", "co"), ("yh", "yl", "xl"))
    return jax.shard_map(shards, mesh=split, in_specs=(placed,), out_specs=placed, check_vma=False)
```

```python
import itertools

import jax
import jax.numpy as jnp
from jax import lax
from jax.experimental import pallas as pl
from jax.experimental.pallas import tpu as pltpu
from jax.sharding import Mesh, PartitionSpec as P

AXES = ("xh", "z", "co", "yh", "yl", "xl")
SIZES = (2, 16, 2, 2, 2, 2)
ROWS = 96
HALF = 48
INFO = 16
DEPTH = 1024
PLANES = 16
GROUP = 4
GROUPS = PLANES // GROUP
WIDTH = GROUP * HALF
EPS = 1e-06
LANES = 128
TILES = DEPTH // LANES
TALL = TILES * HALF
TOP = 16384.0
FIRST_EXPONENT = 7
NORM_UNIT = 32.0
LIFT = 16384.0


def wide(left, right):
    return lax.dot_general(left, right, (((1,), (1,)), ((), ())), preferred_element_type=jnp.float32)


def on_diagonal(rows, lanes, shift=0):
    row = lax.broadcasted_iota(jnp.int32, (rows, lanes), 0)
    return row + shift == lax.broadcasted_iota(jnp.int32, (rows, lanes), 1)


def rounded(x):
    return x.astype(jnp.bfloat16).astype(jnp.float32)


def three_parts(along):
    high = rounded(along)
    middle = rounded((along - high) * 256.0)
    low = rounded((along - high - middle * (1.0 / 256.0)) * 65536.0)
    return high, middle, low


def stacked(parts, rows, lanes):
    row = lax.broadcasted_iota(jnp.int32, (rows, lanes), 0)
    out = jnp.zeros((rows, lanes), jnp.float32)
    for i, part in enumerate(parts):
        out = jnp.where(row == i, part, out)
    return out


def exponent_for(largest):
    scale = jnp.full(largest.shape, 2.0**FIRST_EXPONENT, jnp.float32)
    exponent = jnp.full(largest.shape, float(FIRST_EXPONENT), jnp.float32)
    for bit in (32, 16, 8, 4, 2, 1):
        fits = largest * scale * 2.0**bit < TOP
        scale = jnp.where(fits, scale * 2.0**bit, scale)
        exponent = jnp.where(fits, exponent + bit, exponent)
    return scale, exponent


def scale_kernel(yh_ref, x_ref, first_ref, second_ref):
    values = x_ref[...].astype(jnp.float32)
    largest = jnp.max(jnp.max(jnp.abs(values), axis=1, keepdims=True), axis=0, keepdims=True)
    scale, exponent = exponent_for(largest)
    scaled = values * scale
    norms = jnp.sqrt(jnp.sum(scaled * scaled, axis=1, keepdims=True)) * (1.0 / NORM_UNIT)
    infos = []
    for half in range(2):
        at = half * HALF
        along = jnp.sum(
            jnp.where(on_diagonal(HALF, LANES), norms[at : at + HALF], 0.0), axis=0, keepdims=True
        )
        infos.append(stacked((*three_parts(along), exponent), INFO, LANES))
    whole = scaled.astype(jnp.bfloat16)
    flipped = yh_ref[0] == 1

    def fill(ref, half):
        for tile in range(TILES):
            lanes = slice(tile * LANES, (tile + 1) * LANES)
            ref[tile * HALF : (tile + 1) * HALF] = whole[half * HALF : (half + 1) * HALF, lanes]
        ref[TALL : TALL + INFO] = infos[half].astype(jnp.bfloat16)

    @pl.when(jnp.logical_not(flipped))
    def _():
        fill(first_ref, 0)
        fill(second_ref, 1)

    @pl.when(flipped)
    def _():
        fill(first_ref, 1)
        fill(second_ref, 0)


def scaled_norm(info):
    return (info[0:1] + info[1:2] * (1.0 / 256.0) + info[2:3] * (1.0 / 65536.0)) * NORM_UNIT


def inverse(norm):
    return jnp.where(norm > 0.0, 1.0 / jnp.where(norm > 0.0, norm, 1.0), 0.0)


def encoded(norm):
    scale, exponent = exponent_for(norm * (1.0 / NORM_UNIT))
    return (*three_parts(norm * scale * (1.0 / NORM_UNIT)), exponent)


def partial_kernel(xh_ref, rows_ref, cols_ref, info_ref, out_ref, left_ref, right_ref, lanes_ref):
    xh = xh_ref[0]
    squares = []
    for row in range(4):
        both = []
        for i, yh in enumerate((xh, 1 - xh)):
            block = rows_ref[2 * row + yh]
            left_ref[i, row * ROWS : (row + 1) * ROWS] = block
            full = block.astype(jnp.float32)
            both.append(jnp.sum(full * full, axis=1, keepdims=True))
        squares.append(both[0] + both[1])
    for z in range(PLANES):
        lanes_ref[0:8, z * HALF : (z + 1) * HALF] = info_ref[z, 0:8, 0:HALF]
        for i, tile in itertools.product(range(2), range(TILES)):
            place = right_ref.at[i, z * HALF : (z + 1) * HALF, tile * LANES : (tile + 1) * LANES]
            at = i * TALL + tile * HALF
            place[...] = cols_ref[z, at : at + HALF]
    gram, col_squares = None, None
    for i in range(2):
        info = lanes_ref[4 * i : 4 * i + 4]
        back = jnp.exp2(-info[3:4])
        norm = scaled_norm(info) * back
        product = wide(left_ref[i], right_ref[i]) * back
        gram = product if gram is None else gram + product
        col_squares = norm * norm if col_squares is None else col_squares + norm * norm
    col_norms = jnp.sqrt(col_squares)
    gram = gram * (inverse(col_norms) * LIFT)
    col_info = stacked(encoded(col_norms), 4, PLANES * HALF)
    for row in range(4):
        row_norms = jnp.sqrt(squares[row])
        scaled = gram[row * ROWS : (row + 1) * ROWS] * inverse(row_norms)
        along = jnp.sum(jnp.where(on_diagonal(ROWS, LANES), row_norms, 0.0), axis=0, keepdims=True)
        row_info = stacked(encoded(along), 4, LANES)
        for group in range(GROUPS):
            slot = row * GROUPS + group
            at = group * WIDTH
            for half in range(2):
                lanes = slice(half * WIDTH, (half + 1) * WIDTH)
                out_ref[slot, 0:HALF, lanes] = scaled[half * HALF : (half + 1) * HALF, at : at + WIDTH]
                out_ref[slot, HALF : HALF + 4, lanes] = col_info[:, at : at + WIDTH]
            out_ref[slot, HALF + 4 : HALF + 8, 0:LANES] = row_info


def final_kernel(parts_ref, out_ref):
    left = lax.broadcasted_iota(jnp.int32, (HALF, 2 * WIDTH), 1) < WIDTH

    def weights(slots, first, lanes):
        infos = [parts_ref[slot, first : first + 4, 0:lanes] for slot in slots]
        norms = [scaled_norm(info) * jnp.exp2(-info[3:4]) for info in infos]
        total = norms[0] * norms[0]
        for norm in norms[1:]:
            total += norm * norm
        shrink = lax.rsqrt(total + EPS) * LIFT**-0.5
        return [norm * shrink for norm in norms]

    downs = []
    for along in weights(range(4), HALF + 4, LANES):
        top, bottom = [
            jnp.sum(jnp.where(on_diagonal(HALF, LANES, at), along, 0.0), axis=1, keepdims=True) for at in (0, HALF)
        ]
        downs.append(jnp.where(left, top, bottom))
    for xh in range(2):
        for core in range(2):
            slots = [(xh * 2 + core) * 4 + low for low in range(4)]
            total = None
            for slot, down, across in zip(slots, downs, weights(slots, HALF, 2 * WIDTH)):
                term = parts_ref[slot, 0:HALF] * down * across
                total = term if total is None else total + term
            for low in range(GROUP):
                at = (low * 2 + core) * ROWS + xh * HALF
                for half in range(2):
                    source = half * WIDTH + low * HALF
                    out_ref[half * HALF : (half + 1) * HALF, at : at + HALF] = total[:, source : source + HALF]


def shards(features):
    in_vmem = pl.BlockSpec(memory_space=pltpu.VMEM)
    in_smem = pl.BlockSpec(memory_space=pltpu.SMEM)
    params = pltpu.CompilerParams(vmem_limit_bytes=40 << 20)
    xh, yh = (lax.axis_index(name).astype(jnp.int32).reshape(1) for name in ("xh", "yh"))
    half_block = jax.ShapeDtypeStruct((TALL + INFO, LANES), jnp.bfloat16)
    first, second = pl.pallas_call(
        scale_kernel,
        out_shape=(half_block, half_block),
        in_specs=[in_smem, in_vmem],
        out_specs=(in_vmem, in_vmem),
        compiler_params=params,
    )(yh, features)
    firsts, seconds = [], []
    for a, b, yl in itertools.product(range(2), repeat=3):
        to = yl if a == b else 1 - yl
        firsts.append((4 * a + 2 * b + yl, 4 * b + 2 * a + to))
        seconds.append((4 * a + 2 * b + yl, 4 * (1 - b) + 2 * a + to))
    first = lax.ppermute(first, ("xh", "yh", "yl"), firsts)
    second = lax.ppermute(second, ("xh", "yh", "yl"), seconds)
    groups = [
        [8 * a + 4 * c + 2 * b + (b ^ mirror) for a, c, b in itertools.product(range(2), repeat=3)]
        for mirror in range(2)
    ]
    rows = lax.all_to_all(
        jnp.broadcast_to(features, (8, ROWS, DEPTH)), ("xh", "co", "yh", "yl"), 0, 0, axis_index_groups=groups
    )
    block = jnp.concatenate([first[:TALL], second[:TALL], first[TALL : TALL + 4], second[TALL : TALL + 4]], axis=0)
    columns = lax.all_gather(block.astype(jnp.float16), "z", axis=0, tiled=False)
    info = columns[:, 2 * TALL :].astype(jnp.float32)
    parts = pl.pallas_call(
        partial_kernel,
        out_shape=jax.ShapeDtypeStruct((4 * GROUPS, HALF + 8, 2 * WIDTH), jnp.float32),
        in_specs=[in_smem] + [in_vmem] * 3,
        out_specs=in_vmem,
        scratch_shapes=[
            pltpu.VMEM((2, 4 * ROWS, DEPTH), jnp.bfloat16),
            pltpu.VMEM((2, PLANES * HALF, DEPTH), jnp.bfloat16),
            pltpu.VMEM((8, PLANES * HALF), jnp.float32),
        ],
        compiler_params=params,
    )(xh, rows, columns.astype(jnp.bfloat16), info)
    parts = lax.all_to_all(parts.astype(jnp.float16), ("xh", "co", "yl", "xl"), 0, 0)
    return pl.pallas_call(
        final_kernel,
        out_shape=jax.ShapeDtypeStruct((ROWS, 4 * WIDTH), jnp.float32),
        in_specs=[in_vmem],
        out_specs=in_vmem,
        compiler_params=params,
    )(parts.astype(jnp.float32))


def solution(mesh):
    split = Mesh(mesh.devices.reshape(SIZES), AXES)
    placed = P(("xh", "z", "co"), ("yh", "yl", "xl"))
    return jax.shard_map(shards, mesh=split, in_specs=(placed,), out_specs=placed, check_vma=False)
```

```python
import itertools

import jax
import jax.numpy as jnp
from jax import lax
from jax.experimental import pallas as pl
from jax.experimental.pallas import tpu as pltpu
from jax.sharding import Mesh, PartitionSpec as P

AXES = ("xh", "z", "co", "yh", "yl", "xl")
SIZES = (2, 16, 2, 2, 2, 2)
ROWS = 96
HALF = 48
INFO = 16
DEPTH = 1024
PLANES = 16
GROUP = 4
GROUPS = PLANES // GROUP
WIDTH = GROUP * HALF
EPS = 1e-06
LANES = 128
TILES = DEPTH // LANES
TALL = TILES * HALF
TOP = 16384.0
FIRST_EXPONENT = 7
NORM_UNIT = 32.0
LIFT = 16384.0


def wide(left, right):
    return lax.dot_general(left, right, (((1,), (1,)), ((), ())), preferred_element_type=jnp.float32)


def on_diagonal(rows, lanes, shift=0):
    row = lax.broadcasted_iota(jnp.int32, (rows, lanes), 0)
    return row + shift == lax.broadcasted_iota(jnp.int32, (rows, lanes), 1)


def rounded(x):
    return x.astype(jnp.bfloat16).astype(jnp.float32)


def three_parts(along):
    high = rounded(along)
    middle = rounded((along - high) * 256.0)
    low = rounded((along - high - middle * (1.0 / 256.0)) * 65536.0)
    return high, middle, low


def stacked(parts, rows, lanes):
    row = lax.broadcasted_iota(jnp.int32, (rows, lanes), 0)
    out = jnp.zeros((rows, lanes), jnp.float32)
    for i, part in enumerate(parts):
        out = jnp.where(row == i, part, out)
    return out


def exponent_for(largest):
    scale = jnp.full(largest.shape, 2.0**FIRST_EXPONENT, jnp.float32)
    exponent = jnp.full(largest.shape, float(FIRST_EXPONENT), jnp.float32)
    for bit in (32, 16, 8, 4, 2, 1):
        fits = largest * scale * 2.0**bit < TOP
        scale = jnp.where(fits, scale * 2.0**bit, scale)
        exponent = jnp.where(fits, exponent + bit, exponent)
    return scale, exponent


def scale_kernel(yh_ref, x_ref, first_ref, second_ref):
    values = x_ref[...].astype(jnp.float32)
    largest = jnp.max(jnp.max(jnp.abs(values), axis=1, keepdims=True), axis=0, keepdims=True)
    scale, exponent = exponent_for(largest)
    scaled = values * scale
    norms = jnp.sqrt(jnp.sum(scaled * scaled, axis=1, keepdims=True)) * (1.0 / NORM_UNIT)
    infos = []
    for half in range(2):
        at = half * HALF
        along = jnp.sum(
            jnp.where(on_diagonal(HALF, LANES), norms[at : at + HALF], 0.0), axis=0, keepdims=True
        )
        infos.append(stacked((*three_parts(along), exponent), INFO, LANES))
    whole = scaled.astype(jnp.bfloat16)
    flipped = yh_ref[0] == 1

    def fill(ref, half):
        for tile in range(TILES):
            lanes = slice(tile * LANES, (tile + 1) * LANES)
            ref[tile * HALF : (tile + 1) * HALF] = whole[half * HALF : (half + 1) * HALF, lanes]
        ref[TALL : TALL + INFO] = infos[half].astype(jnp.bfloat16)

    @pl.when(jnp.logical_not(flipped))
    def _():
        fill(first_ref, 0)
        fill(second_ref, 1)

    @pl.when(flipped)
    def _():
        fill(first_ref, 1)
        fill(second_ref, 0)


def scaled_norm(info):
    return (info[0:1] + info[1:2] * (1.0 / 256.0) + info[2:3] * (1.0 / 65536.0)) * NORM_UNIT


def inverse(norm):
    return jnp.where(norm > 0.0, 1.0 / jnp.where(norm > 0.0, norm, 1.0), 0.0)


def encoded(norm):
    scale, exponent = exponent_for(norm * (1.0 / NORM_UNIT))
    return (*three_parts(norm * scale * (1.0 / NORM_UNIT)), exponent)


def partial_kernel(xh_ref, rows_ref, cols_ref, info_ref, out_ref, left_ref, right_ref, lanes_ref, sems):
    xh = xh_ref[0]
    copies = [
        [
            pltpu.make_async_copy(
                rows_ref.at[2 * row + yh], left_ref.at[i, pl.ds(row * ROWS, ROWS)], sems.at[i, row]
            )
            for row in range(4)
        ]
        for i, yh in enumerate((xh, 1 - xh))
    ]
    for copy in copies[0] + copies[1]:
        copy.start()
    for z in range(PLANES):
        lanes_ref[0:8, z * HALF : (z + 1) * HALF] = info_ref[z, 0:8, 0:HALF]
        for i, tile in itertools.product(range(2), range(TILES)):
            place = right_ref.at[i, z * HALF : (z + 1) * HALF, tile * LANES : (tile + 1) * LANES]
            at = i * TALL + tile * HALF
            place[...] = cols_ref[z, at : at + HALF]
    gram, col_squares, squares = None, None, None
    for i in range(2):
        for copy in copies[i]:
            copy.wait()
        full = left_ref[i].astype(jnp.float32)
        square = jnp.sum(full * full, axis=1, keepdims=True)
        squares = square if squares is None else squares + square
        info = lanes_ref[4 * i : 4 * i + 4]
        back = jnp.exp2(-info[3:4])
        norm = scaled_norm(info) * back
        product = wide(left_ref[i], right_ref[i]) * back
        gram = product if gram is None else gram + product
        col_squares = norm * norm if col_squares is None else col_squares + norm * norm
    col_norms = jnp.sqrt(col_squares)
    gram = gram * (inverse(col_norms) * LIFT)
    col_info = stacked(encoded(col_norms), 4, PLANES * HALF)
    for row in range(4):
        row_norms = jnp.sqrt(squares[row * ROWS : (row + 1) * ROWS])
        scaled = gram[row * ROWS : (row + 1) * ROWS] * inverse(row_norms)
        along = jnp.sum(jnp.where(on_diagonal(ROWS, LANES), row_norms, 0.0), axis=0, keepdims=True)
        row_info = stacked(encoded(along), 4, LANES)
        for group in range(GROUPS):
            slot = row * GROUPS + group
            at = group * WIDTH
            for half in range(2):
                lanes = slice(half * WIDTH, (half + 1) * WIDTH)
                out_ref[slot, 0:HALF, lanes] = scaled[half * HALF : (half + 1) * HALF, at : at + WIDTH]
                out_ref[slot, HALF : HALF + 4, lanes] = col_info[:, at : at + WIDTH]
            out_ref[slot, HALF + 4 : HALF + 8, 0:LANES] = row_info


def final_kernel(parts_ref, out_ref):
    left = lax.broadcasted_iota(jnp.int32, (HALF, 2 * WIDTH), 1) < WIDTH

    def weights(slots, first, lanes):
        infos = [parts_ref[slot, first : first + 4, 0:lanes] for slot in slots]
        norms = [scaled_norm(info) * jnp.exp2(-info[3:4]) for info in infos]
        total = norms[0] * norms[0]
        for norm in norms[1:]:
            total += norm * norm
        shrink = lax.rsqrt(total + EPS) * LIFT**-0.5
        return [norm * shrink for norm in norms]

    downs = []
    for along in weights(range(4), HALF + 4, LANES):
        top, bottom = [
            jnp.sum(jnp.where(on_diagonal(HALF, LANES, at), along, 0.0), axis=1, keepdims=True) for at in (0, HALF)
        ]
        downs.append(jnp.where(left, top, bottom))
    for xh in range(2):
        for core in range(2):
            slots = [(xh * 2 + core) * 4 + low for low in range(4)]
            total = None
            for slot, down, across in zip(slots, downs, weights(slots, HALF, 2 * WIDTH)):
                term = parts_ref[slot, 0:HALF] * down * across
                total = term if total is None else total + term
            for low in range(GROUP):
                at = (low * 2 + core) * ROWS + xh * HALF
                for half in range(2):
                    source = half * WIDTH + low * HALF
                    out_ref[half * HALF : (half + 1) * HALF, at : at + HALF] = total[:, source : source + HALF]


def shards(features):
    in_vmem = pl.BlockSpec(memory_space=pltpu.VMEM)
    in_smem = pl.BlockSpec(memory_space=pltpu.SMEM)
    params = pltpu.CompilerParams(vmem_limit_bytes=40 << 20)
    xh, yh = (lax.axis_index(name).astype(jnp.int32).reshape(1) for name in ("xh", "yh"))
    half_block = jax.ShapeDtypeStruct((TALL + INFO, LANES), jnp.bfloat16)
    first, second = pl.pallas_call(
        scale_kernel,
        out_shape=(half_block, half_block),
        in_specs=[in_smem, in_vmem],
        out_specs=(in_vmem, in_vmem),
        compiler_params=params,
    )(yh, features)
    firsts, seconds = [], []
    for a, b, yl in itertools.product(range(2), repeat=3):
        to = yl if a == b else 1 - yl
        firsts.append((4 * a + 2 * b + yl, 4 * b + 2 * a + to))
        seconds.append((4 * a + 2 * b + yl, 4 * (1 - b) + 2 * a + to))
    first = lax.ppermute(first, ("xh", "yh", "yl"), firsts)
    second = lax.ppermute(second, ("xh", "yh", "yl"), seconds)
    groups = [
        [8 * a + 4 * c + 2 * b + (b ^ mirror) for a, c, b in itertools.product(range(2), repeat=3)]
        for mirror in range(2)
    ]
    rows = lax.all_to_all(
        jnp.broadcast_to(features, (8, ROWS, DEPTH)), ("xh", "co", "yh", "yl"), 0, 0, axis_index_groups=groups
    )
    block = jnp.concatenate([first[:TALL], second[:TALL], first[TALL : TALL + 4], second[TALL : TALL + 4]], axis=0)
    columns = lax.all_gather(block.astype(jnp.float16), "z", axis=0, tiled=False)
    info = columns[:, 2 * TALL :].astype(jnp.float32)
    parts = pl.pallas_call(
        partial_kernel,
        out_shape=jax.ShapeDtypeStruct((4 * GROUPS, HALF + 8, 2 * WIDTH), jnp.float32),
        in_specs=[in_smem, pl.BlockSpec(memory_space=pl.ANY), in_vmem, in_vmem],
        out_specs=in_vmem,
        scratch_shapes=[
            pltpu.VMEM((2, 4 * ROWS, DEPTH), jnp.bfloat16),
            pltpu.VMEM((2, PLANES * HALF, DEPTH), jnp.bfloat16),
            pltpu.VMEM((8, PLANES * HALF), jnp.float32),
            pltpu.SemaphoreType.DMA((2, 4)),
        ],
        compiler_params=params,
    )(xh, rows, columns.astype(jnp.bfloat16), info)
    parts = lax.all_to_all(parts.astype(jnp.float16), ("xh", "co", "yl", "xl"), 0, 0)
    return pl.pallas_call(
        final_kernel,
        out_shape=jax.ShapeDtypeStruct((ROWS, 4 * WIDTH), jnp.float32),
        in_specs=[in_vmem],
        out_specs=in_vmem,
        compiler_params=params,
    )(parts.astype(jnp.float32))


def solution(mesh):
    split = Mesh(mesh.devices.reshape(SIZES), AXES)
    placed = P(("xh", "z", "co"), ("yh", "yl", "xl"))
    return jax.shard_map(shards, mesh=split, in_specs=(placed,), out_specs=placed, check_vma=False)
```

```python
import itertools

import jax
import jax.numpy as jnp
from jax import lax
from jax.experimental import pallas as pl
from jax.experimental.pallas import tpu as pltpu
from jax.sharding import Mesh, PartitionSpec as P

AXES = ("xh", "z", "co", "yh", "yl", "xl")
SIZES = (2, 16, 2, 2, 2, 2)
ROWS = 96
HALF = 48
INFO = 16
DEPTH = 1024
PLANES = 16
GROUP = 4
GROUPS = PLANES // GROUP
WIDTH = GROUP * HALF
EPS = 1e-06
LANES = 128
TILES = DEPTH // LANES
TALL = TILES * HALF
TOP = 16384.0
FIRST_EXPONENT = 7
NORM_UNIT = 32.0
LIFT = 16384.0


def wide(left, right):
    return lax.dot_general(left, right, (((1,), (1,)), ((), ())), preferred_element_type=jnp.float32)


def on_diagonal(rows, lanes, shift=0):
    row = lax.broadcasted_iota(jnp.int32, (rows, lanes), 0)
    return row + shift == lax.broadcasted_iota(jnp.int32, (rows, lanes), 1)


def rounded(x):
    return x.astype(jnp.bfloat16).astype(jnp.float32)


def three_parts(along):
    high = rounded(along)
    middle = rounded((along - high) * 256.0)
    low = rounded((along - high - middle * (1.0 / 256.0)) * 65536.0)
    return high, middle, low


def stacked(parts, rows, lanes):
    row = lax.broadcasted_iota(jnp.int32, (rows, lanes), 0)
    out = jnp.zeros((rows, lanes), jnp.float32)
    for i, part in enumerate(parts):
        out = jnp.where(row == i, part, out)
    return out


def exponent_for(largest):
    scale = jnp.full(largest.shape, 2.0**FIRST_EXPONENT, jnp.float32)
    exponent = jnp.full(largest.shape, float(FIRST_EXPONENT), jnp.float32)
    for bit in (32, 16, 8, 4, 2, 1):
        fits = largest * scale * 2.0**bit < TOP
        scale = jnp.where(fits, scale * 2.0**bit, scale)
        exponent = jnp.where(fits, exponent + bit, exponent)
    return scale, exponent


def scale_kernel(yh_ref, x_ref, first_ref, second_ref):
    values = x_ref[...].astype(jnp.float32)
    largest = jnp.max(jnp.max(jnp.abs(values), axis=1, keepdims=True), axis=0, keepdims=True)
    scale, exponent = exponent_for(largest)
    scaled = values * scale
    norms = jnp.sqrt(jnp.sum(scaled * scaled, axis=1, keepdims=True)) * (1.0 / NORM_UNIT)
    infos = []
    for half in range(2):
        at = half * HALF
        along = jnp.sum(
            jnp.where(on_diagonal(HALF, LANES), norms[at : at + HALF], 0.0), axis=0, keepdims=True
        )
        infos.append(stacked((*three_parts(along), exponent), INFO, LANES))
    whole = scaled.astype(jnp.bfloat16)
    flipped = yh_ref[0] == 1

    def fill(ref, half):
        for tile in range(TILES):
            lanes = slice(tile * LANES, (tile + 1) * LANES)
            ref[tile * HALF : (tile + 1) * HALF] = whole[half * HALF : (half + 1) * HALF, lanes]
        ref[TALL : TALL + INFO] = infos[half].astype(jnp.bfloat16)

    @pl.when(jnp.logical_not(flipped))
    def _():
        fill(first_ref, 0)
        fill(second_ref, 1)

    @pl.when(flipped)
    def _():
        fill(first_ref, 1)
        fill(second_ref, 0)


def copies_kernel(x_ref, out_ref, sems):
    copies = [pltpu.make_async_copy(x_ref, out_ref.at[i], sems.at[i]) for i in range(8)]
    for copy in copies:
        copy.start()
    for copy in copies:
        copy.wait()


def scaled_norm(info):
    return (info[0:1] + info[1:2] * (1.0 / 256.0) + info[2:3] * (1.0 / 65536.0)) * NORM_UNIT


def inverse(norm):
    return jnp.where(norm > 0.0, 1.0 / jnp.where(norm > 0.0, norm, 1.0), 0.0)


def encoded(norm):
    scale, exponent = exponent_for(norm * (1.0 / NORM_UNIT))
    return (*three_parts(norm * scale * (1.0 / NORM_UNIT)), exponent)


def partial_kernel(xh_ref, rows_ref, cols_ref, info_ref, out_ref, left_ref, right_ref, lanes_ref):
    xh = xh_ref[0]
    squares = []
    for row in range(4):
        both = []
        for i, yh in enumerate((xh, 1 - xh)):
            block = rows_ref[2 * row + yh]
            left_ref[i, row * ROWS : (row + 1) * ROWS] = block
            full = block.astype(jnp.float32)
            both.append(jnp.sum(full * full, axis=1, keepdims=True))
        squares.append(both[0] + both[1])
    for z in range(PLANES):
        lanes_ref[0:8, z * HALF : (z + 1) * HALF] = info_ref[z, 0:8, 0:HALF]
        for i, tile in itertools.product(range(2), range(TILES)):
            place = right_ref.at[i, z * HALF : (z + 1) * HALF, tile * LANES : (tile + 1) * LANES]
            at = i * TALL + tile * HALF
            place[...] = cols_ref[z, at : at + HALF]
    gram, col_squares = None, None
    for i in range(2):
        info = lanes_ref[4 * i : 4 * i + 4]
        back = jnp.exp2(-info[3:4])
        norm = scaled_norm(info) * back
        product = wide(left_ref[i], right_ref[i]) * back
        gram = product if gram is None else gram + product
        col_squares = norm * norm if col_squares is None else col_squares + norm * norm
    col_norms = jnp.sqrt(col_squares)
    gram = gram * (inverse(col_norms) * LIFT)
    col_info = stacked(encoded(col_norms), 4, PLANES * HALF)
    for row in range(4):
        row_norms = jnp.sqrt(squares[row])
        scaled = gram[row * ROWS : (row + 1) * ROWS] * inverse(row_norms)
        along = jnp.sum(jnp.where(on_diagonal(ROWS, LANES), row_norms, 0.0), axis=0, keepdims=True)
        row_info = stacked(encoded(along), 4, LANES)
        for group in range(GROUPS):
            slot = row * GROUPS + group
            at = group * WIDTH
            for half in range(2):
                lanes = slice(half * WIDTH, (half + 1) * WIDTH)
                out_ref[slot, 0:HALF, lanes] = scaled[half * HALF : (half + 1) * HALF, at : at + WIDTH]
                out_ref[slot, HALF : HALF + 4, lanes] = col_info[:, at : at + WIDTH]
            out_ref[slot, HALF + 4 : HALF + 8, 0:LANES] = row_info


def final_kernel(parts_ref, out_ref):
    left = lax.broadcasted_iota(jnp.int32, (HALF, 2 * WIDTH), 1) < WIDTH

    def weights(slots, first, lanes):
        infos = [parts_ref[slot, first : first + 4, 0:lanes] for slot in slots]
        norms = [scaled_norm(info) * jnp.exp2(-info[3:4]) for info in infos]
        total = norms[0] * norms[0]
        for norm in norms[1:]:
            total += norm * norm
        shrink = lax.rsqrt(total + EPS) * LIFT**-0.5
        return [norm * shrink for norm in norms]

    downs = []
    for along in weights(range(4), HALF + 4, LANES):
        top, bottom = [
            jnp.sum(jnp.where(on_diagonal(HALF, LANES, at), along, 0.0), axis=1, keepdims=True) for at in (0, HALF)
        ]
        downs.append(jnp.where(left, top, bottom))
    for xh in range(2):
        for core in range(2):
            slots = [(xh * 2 + core) * 4 + low for low in range(4)]
            total = None
            for slot, down, across in zip(slots, downs, weights(slots, HALF, 2 * WIDTH)):
                term = parts_ref[slot, 0:HALF] * down * across
                total = term if total is None else total + term
            for low in range(GROUP):
                at = (low * 2 + core) * ROWS + xh * HALF
                for half in range(2):
                    source = half * WIDTH + low * HALF
                    out_ref[half * HALF : (half + 1) * HALF, at : at + HALF] = total[:, source : source + HALF]


def shards(features):
    in_vmem = pl.BlockSpec(memory_space=pltpu.VMEM)
    in_smem = pl.BlockSpec(memory_space=pltpu.SMEM)
    params = pltpu.CompilerParams(vmem_limit_bytes=40 << 20)
    xh, yh = (lax.axis_index(name).astype(jnp.int32).reshape(1) for name in ("xh", "yh"))
    half_block = jax.ShapeDtypeStruct((TALL + INFO, LANES), jnp.bfloat16)
    first, second = pl.pallas_call(
        scale_kernel,
        out_shape=(half_block, half_block),
        in_specs=[in_smem, in_vmem],
        out_specs=(in_vmem, in_vmem),
        compiler_params=params,
    )(yh, features)
    firsts, seconds = [], []
    for a, b, yl in itertools.product(range(2), repeat=3):
        to = yl if a == b else 1 - yl
        firsts.append((4 * a + 2 * b + yl, 4 * b + 2 * a + to))
        seconds.append((4 * a + 2 * b + yl, 4 * (1 - b) + 2 * a + to))
    first = lax.ppermute(first, ("xh", "yh", "yl"), firsts)
    second = lax.ppermute(second, ("xh", "yh", "yl"), seconds)
    groups = [
        [8 * a + 4 * c + 2 * b + (b ^ mirror) for a, c, b in itertools.product(range(2), repeat=3)]
        for mirror in range(2)
    ]
    copies = pl.pallas_call(
        copies_kernel,
        out_shape=jax.ShapeDtypeStruct((8, ROWS, DEPTH), jnp.bfloat16),
        in_specs=[in_vmem],
        out_specs=pl.BlockSpec(memory_space=pl.ANY),
        scratch_shapes=[pltpu.SemaphoreType.DMA((8,))],
        compiler_params=params,
    )(features)
    rows = lax.all_to_all(
        copies, ("xh", "co", "yh", "yl"), 0, 0, axis_index_groups=groups
    )
    block = jnp.concatenate([first[:TALL], second[:TALL], first[TALL : TALL + 4], second[TALL : TALL + 4]], axis=0)
    columns = lax.all_gather(block.astype(jnp.float16), "z", axis=0, tiled=False)
    info = columns[:, 2 * TALL :].astype(jnp.float32)
    parts = pl.pallas_call(
        partial_kernel,
        out_shape=jax.ShapeDtypeStruct((4 * GROUPS, HALF + 8, 2 * WIDTH), jnp.float32),
        in_specs=[in_smem] + [in_vmem] * 3,
        out_specs=in_vmem,
        scratch_shapes=[
            pltpu.VMEM((2, 4 * ROWS, DEPTH), jnp.bfloat16),
            pltpu.VMEM((2, PLANES * HALF, DEPTH), jnp.bfloat16),
            pltpu.VMEM((8, PLANES * HALF), jnp.float32),
        ],
        compiler_params=params,
    )(xh, rows, columns.astype(jnp.bfloat16), info)
    parts = lax.all_to_all(parts.astype(jnp.float16), ("xh", "co", "yl", "xl"), 0, 0)
    return pl.pallas_call(
        final_kernel,
        out_shape=jax.ShapeDtypeStruct((ROWS, 4 * WIDTH), jnp.float32),
        in_specs=[in_vmem],
        out_specs=in_vmem,
        compiler_params=params,
    )(parts.astype(jnp.float32))


def solution(mesh):
    split = Mesh(mesh.devices.reshape(SIZES), AXES)
    placed = P(("xh", "z", "co"), ("yh", "yl", "xl"))
    return jax.shard_map(shards, mesh=split, in_specs=(placed,), out_specs=placed, check_vma=False)
```
